32 devices in a mesh: ens: 2 (over x), fn: 16 (over z, y, core).
Axes of the slice: x: 2, y: 2, z: 4, core: 2. Of those that a mesh axis runs over, the one named last changes fastest.
Arguments:
- sensor_values: bfloat16 [8192, 1024], P(('ens', 'fn')), parts along dimension 0, may hold values from -6 to 6
- amplitude: float32 [8192], P(('ens', 'fn')), parts along dimension 0, may hold values from 0.3 to 1.5
- field_modes: int32 [8192, 2], P(('ens', 'fn')), parts along dimension 0, may hold values from 1 to 5
- point_index: int32 [256, 2], P(('ens', 'fn')), parts along dimension 0, may hold values from 0 to 127
- forcing: bfloat16 [256], P(('ens', 'fn')), parts along dimension 0, may hold values from -6 to 6
- branch_in: bfloat16 [1024, 512], replicated, may hold values from -0.1875 to 0.1875
- branch_in_bias: float32 [512], replicated, may hold values from -3 to 3
- branch_out: bfloat16 [512, 512], replicated, may hold values from -0.046875 to 0.046875
- branch_out_bias: float32 [512], replicated, may hold values from -0.6 to 0.6
- trunk_in: float32 [2, 512], replicated, may hold values from -8 to 8
- trunk_in_bias: float32 [512], replicated, may hold values from -4 to 4
- trunk_out: bfloat16 [512, 512], replicated, may hold values from -0.25 to 0.25
- trunk_out_bias: float32 [512], replicated, may hold values from -3 to 3
Outputs:
- grad_branch_in: float32 [2048, 512], P(('ens', 'fn')), parts along dimension 0
- grad_branch_out: float32 [1024, 512], P(('ens', 'fn')), parts along dimension 0
- grad_trunk_out: float32 [1024, 512], P(('ens', 'fn')), parts along dimension 0
The draws below stay inside these ranges and needn't reach their ends.
There are 2 independent parts, one for each index of `ens`. The reference program is written for one: setup_inputs(seed, part) draws one part's arguments, and reference() takes and returns one part's arrays. A program takes and returns all parts, laid end to end along the dimension named above; an argument that names none is the same for every part. Nothing has to cross between parts.
All inputs are finite; a program needn't handle non-finite values.
Results may differ from the reference program's by a relative error of at most 0.0057.
Values may be sent and summed in bfloat16 or wider, within the bound.
A program may use at most 64 MiB of HBM per device.

```python
import math
import jax
import jax.numpy as jnp
from jax import lax

S = 1024
BH = 512
TH = 512
PW = 512
GRID = 128
F_DEV = 256
FIELDS = 4096
POINTS = 128


def plant(array, stream_key, smallest, high):
    index_at = [jax.random.randint(jax.random.fold_in(stream_key, axis), (), 0, length) for axis, length in enumerate(array.shape)]
    widest = array.shape.index(max(array.shape))
    beside = index_at[:widest] + [(index_at[widest] + 1) % array.shape[widest]] + index_at[widest + 1:]
    return array.at[tuple(index_at)].set(smallest).at[tuple(beside)].set(high)


def raised(entries, rng, source, target, shards_of, factor):
    owner, partner = [(jnp.arange(entries.shape[dim]) // (entries.shape[dim] // shards_of)).reshape([-1 if axis == dim else 1 for axis in range(entries.ndim)]) for dim in (source, target)]
    chosen = jax.random.permutation(rng, shards_of)[partner]
    strong = (owner == chosen) | (owner == (partner + shards_of // 2) % shards_of)
    return jnp.where(strong, factor * entries, entries)


def block_levels(own_key, shape, split, smallest, top_value):
    loudness = 1.0
    for axis_at, blocks in split:
        heights = jax.random.uniform(jax.random.fold_in(jax.random.fold_in(own_key, 6), axis_at), (blocks,), jnp.float32, smallest / len(split), top_value / len(split))
        loudness = loudness * jnp.repeat(jnp.exp(heights), shape[axis_at] // blocks).reshape((-1,) + (1,) * (len(shape) - 1 - axis_at))
    return loudness


def noise(rng, shape, scale, reach, split=(), held_as=jnp.bfloat16):
    entries = jax.random.normal(rng, shape, jnp.float32) * scale
    if len(split) > 0:
        entries = block_levels(rng, shape, split, -0.22, 0.18) * entries
    return jnp.clip(entries, min=-reach, max=reach).astype(held_as)


def heavy_noise(own_key, dims, scale, bound, shards, heavy, kind=jnp.bfloat16):
    result = scale * jax.random.normal(own_key, dims, jnp.float32)
    if shards:
        result = result * block_levels(own_key, dims, shards, -0.22, 0.18)
    return jnp.clip(raised(result, jax.random.fold_in(own_key, 3), *heavy), -bound, bound).astype(kind)


def setup_inputs(seed: int = 0, part: int = 0) -> dict:
    key_of = jax.random.split(jax.random.key(seed), 14)
    own_keys = jax.random.split(jax.random.fold_in(key_of[13], part), 14)
    sensor_values = heavy_noise(own_keys[0], (FIELDS, S), 1.0, 6.0, ((0, 16),), (0, 1, 16, 2.0))
    amplitude = jnp.clip(jnp.exp(math.log(1.5) - 1.60943787 * jax.random.uniform(own_keys[1], (FIELDS,), jnp.float32) ** block_levels(own_keys[1], (FIELDS,), ((0, 16),), -0.2, 0.2)), 0.3, 1.5)
    field_modes = plant(jax.random.randint(own_keys[2], (FIELDS, 2), 1, 6), jax.random.fold_in(own_keys[2], 1), 1, 5).astype(jnp.int32)
    point_index = plant(jax.random.randint(own_keys[3], (POINTS, 2), 0, GRID), jax.random.fold_in(own_keys[3], 1), 0, GRID - 1).astype(jnp.int32)
    forcing = noise(own_keys[4], (POINTS,), 1.0, 6.0, ((0, 16),))
    branch_in = noise(key_of[5], (S, BH), S ** -0.5, 0.1875)
    branch_in_bias = noise(key_of[6], (BH,), 0.5, 3.0, (), jnp.float32)
    branch_out = noise(key_of[7], (BH, PW), (BH * PW // 16) ** -0.5, 0.046875)
    branch_out_bias = noise(key_of[8], (PW,), 0.1, 0.6, (), jnp.float32)
    trunk_in = noise(key_of[9], (2, TH), 2.0, 8.0, (), jnp.float32)
    trunk_in_bias = noise(key_of[10], (TH,), 1.0, 4.0, (), jnp.float32)
    trunk_out = noise(key_of[11], (TH, PW), TH ** -0.5, 0.25)
    trunk_out_bias = noise(key_of[12], (PW,), 0.5, 3.0, (), jnp.float32)
    return {"sensor_values": sensor_values, "amplitude": amplitude, "field_modes": field_modes, "point_index": point_index, "forcing": forcing, "branch_in": branch_in, "branch_in_bias": branch_in_bias, "branch_out": branch_out, "branch_out_bias": branch_out_bias, "trunk_in": trunk_in, "trunk_in_bias": trunk_in_bias, "trunk_out": trunk_out, "trunk_out_bias": trunk_out_bias}


def grid_coords(point_index):
    return (point_index.astype(jnp.float32) + 0.5) / GRID


def trunk_hidden(coords, trunk_in, trunk_in_bias):
    pre_act = coords[:, 0:1] * trunk_in[0][None, :] + coords[:, 1:2] * trunk_in[1][None, :] + trunk_in_bias[None, :]
    activ = jnp.tanh(pre_act)
    first_der = 1.0 - activ * activ
    second_der = -2.0 * activ * first_der
    square_sum = trunk_in[0] * trunk_in[0] + trunk_in[1] * trunk_in[1]
    stacked = jnp.stack([activ, first_der * trunk_in[0], first_der * trunk_in[1], second_der * square_sum], axis=1)
    return stacked.astype(jnp.bfloat16)


def trunk_tangents(hidden, trunk_out, trunk_out_bias):
    npts = hidden.shape[0]
    width = trunk_out.shape[1]
    flat_out = jnp.dot(hidden.reshape(npts * 4, hidden.shape[2]), trunk_out, preferred_element_type=jnp.float32)
    chan_mask = (jnp.arange(4) == 0).astype(jnp.float32)
    shaped = flat_out.reshape(npts, 4, width) + chan_mask[None, :, None] * trunk_out_bias[None, None, :]
    return shaped.astype(jnp.bfloat16)


def tile_cotangent(branch_feat, tangents, coords, forcing_pts, amplitude, field_modes):
    npts = tangents.shape[0]
    nfield = branch_feat.shape[0]
    flattened = tangents.reshape(npts * 4, tangents.shape[2])
    tile_vals = lax.dot_general(branch_feat, flattened, (((1,), (1,)), ((), ())), preferred_element_type=jnp.float32)
    tile_vals = tile_vals.reshape(nfield, npts, 4)
    x_coord = coords[:, 0][None, :]
    y_coord = coords[:, 1][None, :]
    freq_x = field_modes[:, 0:1].astype(jnp.float32) * math.pi
    freq_y = field_modes[:, 1:2].astype(jnp.float32) * math.pi
    amp_col = amplitude[:, None]
    sin_x = jnp.sin(freq_x * x_coord)
    cos_x = jnp.cos(freq_x * x_coord)
    sin_y = jnp.sin(freq_y * y_coord)
    cos_y = jnp.cos(freq_y * y_coord)
    perm = jnp.exp(amp_col * sin_x * sin_y)
    perm_dx = perm * amp_col * freq_x * cos_x * sin_y
    perm_dy = perm * amp_col * freq_y * sin_x * cos_y
    residual_tile = tile_vals[:, :, 0] - (perm * tile_vals[:, :, 3] + perm_dx * tile_vals[:, :, 1] + perm_dy * tile_vals[:, :, 2]) - forcing_pts.astype(jnp.float32)[None, :]
    scaled = residual_tile / npts
    stacked = jnp.stack([scaled, -scaled * perm_dx, -scaled * perm_dy, -scaled * perm], axis=2)
    return stacked.astype(jnp.bfloat16).reshape(nfield, npts * 4)


def reference(sensor_values, amplitude, field_modes, point_index, forcing, branch_in, branch_in_bias, branch_out, branch_out_bias, trunk_in, trunk_in_bias, trunk_out, trunk_out_bias):
    coords = grid_coords(point_index)
    hidden_all = trunk_hidden(coords, trunk_in, trunk_in_bias)
    tangents = trunk_tangents(hidden_all, trunk_out, trunk_out_bias)
    flattened = tangents.reshape(POINTS * 4, PW)
    nblocks = FIELDS // F_DEV

    def one_block(totals, block_inputs):
        sensors_blk, amp_blk, modes_blk = block_inputs
        branch_hidden = jnp.tanh(jnp.dot(sensors_blk, branch_in, preferred_element_type=jnp.float32) + branch_in_bias[None, :]).astype(jnp.bfloat16)
        branch_feat = (jnp.dot(branch_hidden, branch_out, preferred_element_type=jnp.float32) + branch_out_bias[None, :]).astype(jnp.bfloat16)
        cotangent = tile_cotangent(branch_feat, tangents, coords, forcing, amp_blk, modes_blk)
        d_branch = jnp.dot(cotangent, flattened, preferred_element_type=jnp.float32).astype(jnp.bfloat16)
        d_tang = lax.dot_general(cotangent, branch_feat, (((0,), (0,)), ((), ())), preferred_element_type=jnp.float32)
        g_out = lax.dot_general(branch_hidden, d_branch, (((0,), (0,)), ((), ())), preferred_element_type=jnp.float32)
        hidden_f = branch_hidden.astype(jnp.float32)
        d_pre = (lax.dot_general(d_branch, branch_out, (((1,), (1,)), ((), ())), preferred_element_type=jnp.float32) * (1.0 - hidden_f * hidden_f)).astype(jnp.bfloat16)
        g_in = lax.dot_general(sensors_blk, d_pre, (((0,), (0,)), ((), ())), preferred_element_type=jnp.float32)
        return (totals[0] + d_tang, totals[1] + g_in, totals[2] + g_out), None

    block_inputs = (sensor_values.reshape(nblocks, F_DEV, S), amplitude.reshape(nblocks, F_DEV), field_modes.reshape(nblocks, F_DEV, 2))
    start_totals = (jnp.zeros((POINTS * 4, PW), jnp.float32), jnp.zeros((S, BH), jnp.float32), jnp.zeros((BH, PW), jnp.float32))
    totals, _ = lax.scan(one_block, start_totals, block_inputs)
    d_tangents, grad_branch_in, grad_branch_out = totals
    hidden_flat = hidden_all.reshape(POINTS * 4, TH).astype(jnp.float32)
    grad_trunk_out = lax.dot_general(hidden_flat, d_tangents, (((0,), (0,)), ((), ())), precision=lax.Precision.HIGHEST, preferred_element_type=jnp.float32)
    return (grad_branch_in, grad_branch_out, grad_trunk_out)
```

```python
import functools
import math

import jax
import jax.numpy as jnp
from jax import lax
from jax.experimental import pallas as pl
from jax.experimental.pallas import tpu as pltpu
from jax.sharding import PartitionSpec as P

GRID = 128
MODES = 5
MESH = pl.DeviceIdType.MESH
ROW_DIMS = (((0,), (0,)), ((), ()))
COL_DIMS = (((1,), (1,)), ((), ()))


def grid_coords(point_index):
    return (point_index.astype(jnp.float32) + 0.5) / GRID


def trunk_hidden(coords, trunk_in, trunk_in_bias):
    pre_act = (
        coords[:, 0:1] * trunk_in[0][None, :]
        + coords[:, 1:2] * trunk_in[1][None, :]
        + trunk_in_bias[None, :]
    )
    activ = jnp.tanh(pre_act)
    first_der = 1.0 - activ * activ
    second_der = -2.0 * activ * first_der
    square_sum = trunk_in[0] * trunk_in[0] + trunk_in[1] * trunk_in[1]
    stacked = jnp.stack(
        [activ, first_der * trunk_in[0], first_der * trunk_in[1], second_der * square_sum], axis=1
    )
    return stacked.astype(jnp.bfloat16)


def trunk_tangents(hidden, trunk_out, trunk_out_bias):
    npts = hidden.shape[0]
    width = trunk_out.shape[1]
    flat_out = jnp.dot(
        hidden.reshape(npts * 4, hidden.shape[2]), trunk_out, preferred_element_type=jnp.float32
    )
    chan_mask = (jnp.arange(4) == 0).astype(jnp.float32)
    shaped = (
        flat_out.reshape(npts, 4, width) + chan_mask[None, :, None] * trunk_out_bias[None, None, :]
    )
    return shaped.astype(jnp.bfloat16)


def tile_cotangent(branch_feat, tangents, coords, forcing_pts, amplitude, field_modes):
    npts = tangents.shape[0]
    nfield = branch_feat.shape[0]
    flattened = tangents.reshape(npts * 4, tangents.shape[2])
    tile_vals = lax.dot_general(
        branch_feat, flattened, (((1,), (1,)), ((), ())), preferred_element_type=jnp.float32
    )
    tile_vals = tile_vals.reshape(nfield, npts, 4)
    x_coord = coords[:, 0][None, :]
    y_coord = coords[:, 1][None, :]
    freq_x = field_modes[:, 0:1].astype(jnp.float32) * math.pi
    freq_y = field_modes[:, 1:2].astype(jnp.float32) * math.pi
    amp_col = amplitude[:, None]
    sin_x = jnp.sin(freq_x * x_coord)
    cos_x = jnp.cos(freq_x * x_coord)
    sin_y = jnp.sin(freq_y * y_coord)
    cos_y = jnp.cos(freq_y * y_coord)
    perm = jnp.exp(amp_col * sin_x * sin_y)
    perm_dx = perm * amp_col * freq_x * cos_x * sin_y
    perm_dy = perm * amp_col * freq_y * sin_x * cos_y
    residual_tile = (
        tile_vals[:, :, 0]
        - (perm * tile_vals[:, :, 3] + perm_dx * tile_vals[:, :, 1] + perm_dy * tile_vals[:, :, 2])
        - forcing_pts.astype(jnp.float32)[None, :]
    )
    scaled = residual_tile / npts
    stacked = jnp.stack([scaled, -scaled * perm_dx, -scaled * perm_dy, -scaled * perm], axis=2)
    return stacked.astype(jnp.bfloat16).reshape(nfield, npts * 4)


def trunk_weight_grad(hidden_rows, d_tangents):
    upper_part = lax.optimization_barrier(d_tangents.astype(jnp.bfloat16))
    lower_part = (d_tangents - upper_part.astype(jnp.float32)).astype(jnp.bfloat16)
    dims = (((0,), (0,)), ((), ()))
    upper_term = lax.dot_general(hidden_rows, upper_part, dims, preferred_element_type=jnp.float32)
    lower_term = lax.dot_general(hidden_rows, lower_part, dims, preferred_element_type=jnp.float32)
    return upper_term + lower_term


def per_device(
    sensor_values,
    amplitude,
    field_modes,
    point_index,
    forcing,
    branch_in,
    branch_in_bias,
    branch_out,
    branch_out_bias,
    trunk_in,
    trunk_in_bias,
    trunk_out,
    trunk_out_bias,
):
    width = trunk_out.shape[1]
    trunk_width = trunk_out.shape[0]
    branch_hidden = jnp.tanh(
        jnp.dot(sensor_values, branch_in, preferred_element_type=jnp.float32)
        + branch_in_bias[None, :]
    ).astype(jnp.bfloat16)
    branch_feat = (
        jnp.dot(branch_hidden, branch_out, preferred_element_type=jnp.float32)
        + branch_out_bias[None, :]
    ).astype(jnp.bfloat16)
    own_coords = grid_coords(point_index)
    hidden_own = trunk_hidden(own_coords, trunk_in, trunk_in_bias)
    tangents_own = trunk_tangents(hidden_own, trunk_out, trunk_out_bias)
    tangents_all, coords_sent, forcing_all = (
        lax.all_gather(tangents_own, "fn", axis=0, tiled=True),
        lax.all_gather(own_coords.astype(jnp.bfloat16), "fn", axis=0, tiled=True),
        lax.all_gather(forcing, "fn", axis=0, tiled=True),
    )
    coords_all = coords_sent.astype(jnp.float32)
    all_points = tangents_all.shape[0]
    cotangent = tile_cotangent(
        branch_feat, tangents_all, coords_all, forcing_all, amplitude, field_modes
    )
    flattened = tangents_all.reshape(all_points * 4, width)
    d_branch = jnp.dot(cotangent, flattened, preferred_element_type=jnp.float32).astype(
        jnp.bfloat16
    )
    grad_out_part = lax.dot_general(
        branch_hidden, d_branch, (((0,), (0,)), ((), ())), preferred_element_type=jnp.float32
    )
    hidden_f = branch_hidden.astype(jnp.float32)
    d_pre = (
        lax.dot_general(
            d_branch, branch_out, (((1,), (1,)), ((), ())), preferred_element_type=jnp.float32
        )
        * (1.0 - hidden_f * hidden_f)
    ).astype(jnp.bfloat16)
    grad_in_part = lax.dot_general(
        sensor_values, d_pre, (((0,), (0,)), ((), ())), preferred_element_type=jnp.float32
    )
    own_rows = hidden_own.shape[0] * 4
    d_tangents = lax.psum_scatter(
        lax.dot_general(
            cotangent, branch_feat, (((0,), (0,)), ((), ())), preferred_element_type=jnp.float32
        ),
        "fn",
        scatter_dimension=0,
        tiled=True,
    )
    hidden_rows = hidden_own.reshape(own_rows, trunk_width)
    grad_trunk_part = trunk_weight_grad(hidden_rows, d_tangents)
    grad_branch_in, grad_branch_out, grad_trunk_out = (
        lax.psum_scatter(grad_in_part, "fn", scatter_dimension=0, tiled=True),
        lax.psum_scatter(grad_out_part, "fn", scatter_dimension=0, tiled=True),
        lax.psum_scatter(grad_trunk_part, "fn", scatter_dimension=0, tiled=True),
    )
    return (grad_branch_in, grad_branch_out, grad_trunk_out)


def to_column(row, count):
    rows = lax.broadcasted_iota(jnp.int32, (count, count), 0)
    lanes = lax.broadcasted_iota(jnp.int32, (count, count), 1)
    return jnp.sum(jnp.where(rows == lanes, row, 0.0), axis=1, keepdims=True)


def spread_rows(row, lanes):
    return jnp.broadcast_to(row, (lanes, row.shape[1])).T


def pick_mode(modes, table):
    picked = jnp.broadcast_to(table[0:1, :], modes.shape)
    for mode in range(2, MODES + 1):
        picked = jnp.where(modes == float(mode), table[mode - 1 : mode, :], picked)
    return picked


def step_kernel(
    n,
    sensors,
    amplitude,
    modes,
    points,
    forcing,
    branch_in,
    branch_in_bias,
    branch_out,
    branch_out_bias,
    trunk_in,
    trunk_in_bias,
    trunk_out,
    trunk_out_bias,
    grad_in_ref,
    grad_out_ref,
    grad_trunk_ref,
    pts,
    hid,
    tang,
    part,
    wide,
    half_send,
    half_keep,
    quarter_send,
    from_core,
    from_y,
    from_z,
    pts_send,
    pts_recv,
    core_send,
    core_recv,
    y_send,
    y_recv,
    z_send,
    z_recv,
):
    f32, bf16 = jnp.float32, jnp.bfloat16
    me = lax.axis_index("fn")
    nz = n // 4
    core = lax.rem(me, 2)
    y_at = lax.rem(me // 2, 2)
    z_at = me // 4
    other_core = me + 1 - 2 * core
    other_y = me + 2 - 4 * y_at
    own = points.shape[1]
    npts = own * n
    rows = from_z.shape[2]

    barrier = pltpu.get_barrier_semaphore()
    for k in range(1, n):
        pl.semaphore_signal(
            barrier, inc=1, device_id={"fn": lax.rem(me + k, n)}, device_id_type=MESH
        )

    coords = (points[...].astype(f32) + 0.5) / GRID
    lane = lax.broadcasted_iota(jnp.int32, (own, 128), 1)
    pts[me] = jnp.where(
        lane == 0,
        to_column(coords[0:1, :], own),
        jnp.where(
            lane == 1,
            to_column(coords[1:2, :], own),
            to_column(forcing[...].astype(f32), own),
        ),
    )
    hidden = jnp.tanh(
        jnp.dot(sensors[...], branch_in[...], preferred_element_type=f32) + branch_in_bias[...]
    ).astype(bf16)

    pl.semaphore_wait(barrier, n - 1)

    def points_copy(k):
        return pltpu.make_async_remote_copy(
            src_ref=pts.at[me],
            dst_ref=pts.at[me],
            send_sem=pts_send.at[k - 1],
            recv_sem=pts_recv.at[k - 1],
            device_id={"fn": lax.rem(me + k, n)},
            device_id_type=MESH,
        )

    def points_arrival(k):
        source = lax.rem(me + n - k, n)
        return pltpu.make_async_remote_copy(
            src_ref=pts.at[source],
            dst_ref=pts.at[source],
            send_sem=pts_send.at[k - 1],
            recv_sem=pts_recv.at[k - 1],
            device_id={"fn": source},
            device_id_type=MESH,
        )

    for k in range(1, n):
        points_copy(k).start()

    feat = (
        jnp.dot(hidden, branch_out[...], preferred_element_type=f32) + branch_out_bias[...]
    ).astype(bf16)
    fields = feat.shape[0]
    amp = spread_rows(amplitude[...], npts)
    mode_x = spread_rows(modes[0:1, :].astype(f32), npts)
    mode_y = spread_rows(modes[1:2, :].astype(f32), npts)

    for k in range(1, n):
        points_arrival(k).wait_recv()
    columns = pts[...].reshape(npts, 128)
    lines = columns.T
    x_row, y_row, force_row = lines[0:1, :], lines[1:2, :], lines[2:3, :]

    weight_x, weight_y = trunk_in[0:1, :], trunk_in[1:2, :]
    act = jnp.tanh(columns[:, 0:1] * weight_x + columns[:, 1:2] * weight_y + trunk_in_bias[...])
    first = 1.0 - act * act
    second = -2.0 * act * first
    hid[0:npts, :] = act.astype(bf16)
    hid[npts : 2 * npts, :] = (first * weight_x).astype(bf16)
    hid[2 * npts : 3 * npts, :] = (first * weight_y).astype(bf16)
    hid[3 * npts : 4 * npts, :] = (
        second * (weight_x * weight_x + weight_y * weight_y)
    ).astype(bf16)
    flat = jnp.dot(hid[...], trunk_out[...], preferred_element_type=f32)
    tang[0:npts, :] = (flat[0:npts, :] + trunk_out_bias[...]).astype(bf16)
    tang[npts:, :] = flat[npts:, :].astype(bf16)

    tile = lax.dot_general(feat, tang[...], COL_DIMS, preferred_element_type=f32)

    freqs = (lax.broadcasted_iota(jnp.int32, (8, npts), 0) + 1).astype(f32) * math.pi
    sin_x = pick_mode(mode_x, jnp.sin(freqs * x_row))
    cos_x = pick_mode(mode_x, jnp.cos(freqs * x_row))
    sin_y = pick_mode(mode_y, jnp.sin(freqs * y_row))
    cos_y = pick_mode(mode_y, jnp.cos(freqs * y_row))
    perm = jnp.exp(amp * sin_x * sin_y)
    perm_dx = perm * amp * (mode_x * math.pi) * cos_x * sin_y
    perm_dy = perm * amp * (mode_y * math.pi) * sin_x * cos_y
    residual = (
        tile[:, 0:npts]
        - (
            perm * tile[:, 3 * npts :]
            + perm_dx * tile[:, npts : 2 * npts]
            + perm_dy * tile[:, 2 * npts : 3 * npts]
        )
        - force_row
    )
    scaled = residual / npts
    cot = jnp.concatenate(
        [
            scaled.astype(bf16),
            (-scaled * perm_dx).astype(bf16),
            (-scaled * perm_dy).astype(bf16),
            (-scaled * perm).astype(bf16),
        ],
        axis=1,
    )

    def keep(piece, value, chunk, start):
        for d in range(n):
            at = (d % 2) * (n // 2) + ((d // 2) % 2) * nz + d // 4
            block = value[d * chunk + start : d * chunk + start + rows, :]
            wide[piece, at] = block
            part[piece, at] = block.astype(bf16)

    def core_copy(piece):
        return pltpu.make_async_remote_copy(
            src_ref=part.at[piece, pl.ds((1 - core) * (n // 2), n // 2)],
            dst_ref=from_core.at[piece],
            send_sem=core_send.at[piece],
            recv_sem=core_recv.at[piece],
            device_id={"fn": other_core},
            device_id_type=MESH,
        )

    def y_copy(piece):
        return pltpu.make_async_remote_copy(
            src_ref=half_send.at[piece],
            dst_ref=from_y.at[piece],
            send_sem=y_send.at[piece],
            recv_sem=y_recv.at[piece],
            device_id={"fn": other_y},
            device_id_type=MESH,
        )

    def z_copy(piece, k):
        return pltpu.make_async_remote_copy(
            src_ref=quarter_send.at[piece, k - 1],
            dst_ref=from_z.at[piece, k - 1],
            send_sem=z_send.at[piece, k - 1],
            recv_sem=z_recv.at[piece, k - 1],
            device_id={"fn": lax.rem(me + 4 * k, n)},
            device_id_type=MESH,
        )

    def core_to_y(piece):
        core_copy(piece).wait_recv()
        away = (1 - y_at) * nz
        half_send[piece] = (
            wide[piece, pl.ds(core * (n // 2) + away, nz)]
            + from_core[piece, pl.ds(away, nz)].astype(f32)
        ).astype(bf16)
        y_copy(piece).start()
        half_keep[piece] = wide[piece, pl.ds(core * (n // 2) + y_at * nz, nz)] + from_core[
            piece, pl.ds(y_at * nz, nz)
        ].astype(f32)

    def y_to_z(piece):
        y_copy(piece).wait_recv()
        for k in range(1, nz):
            target = lax.rem(z_at + k, nz)
            quarter_send[piece, k - 1] = (
                half_keep[piece, target] + from_y[piece, target].astype(f32)
            ).astype(bf16)
            z_copy(piece, k).start()

    def finish(piece):
        total = half_keep[piece, z_at] + from_y[piece, z_at].astype(f32)
        for k in range(1, nz):
            z_copy(piece, k).wait_recv()
            total = total + from_z[piece, k - 1].astype(f32)
        return total

    trunk_mix = jnp.dot(cot, hid[...], preferred_element_type=f32)
    upper = trunk_mix.astype(bf16)
    lower = (trunk_mix - upper.astype(f32)).astype(bf16)
    grad_trunk = lax.dot_general(
        upper, feat, ROW_DIMS, preferred_element_type=f32
    ) + lax.dot_general(lower, feat, ROW_DIMS, preferred_element_type=f32)
    keep(0, grad_trunk, rows, 0)
    core_copy(0).start()

    d_branch = jnp.dot(cot, tang[...], preferred_element_type=f32).astype(bf16)
    keep(1, lax.dot_general(hidden, d_branch, ROW_DIMS, preferred_element_type=f32), rows, 0)
    core_copy(1).start()
    core_to_y(0)

    hidden_f = hidden.astype(f32)
    d_pre = (
        lax.dot_general(d_branch, branch_out[...], COL_DIMS, preferred_element_type=f32)
        * (1.0 - hidden_f * hidden_f)
    ).astype(bf16)
    grad_in = lax.dot_general(sensors[...], d_pre, ROW_DIMS, preferred_element_type=f32)
    core_to_y(1)
    keep(2, grad_in, 2 * rows, 0)
    core_copy(2).start()
    keep(3, grad_in, 2 * rows, rows)
    core_copy(3).start()
    y_to_z(0)
    core_to_y(2)
    core_to_y(3)
    y_to_z(1)
    y_to_z(2)
    y_to_z(3)
    grad_trunk_ref[...] = finish(0)
    grad_out_ref[...] = finish(1)
    grad_in_ref[0:rows, :] = finish(2)
    grad_in_ref[rows : 2 * rows, :] = finish(3)

    for k in range(1, n):
        points_copy(k).wait_send()
    for piece in range(4):
        core_copy(piece).wait_send()
        y_copy(piece).wait_send()
        for k in range(1, nz):
            z_copy(piece, k).wait_send()


def fused_step(
    n,
    sensor_values,
    amplitude,
    field_modes,
    point_index,
    forcing,
    branch_in,
    branch_in_bias,
    branch_out,
    branch_out_bias,
    trunk_in,
    trunk_in_bias,
    trunk_out,
    trunk_out_bias,
):
    f32, bf16 = jnp.float32, jnp.bfloat16
    sensors = sensor_values.shape[1]
    width = trunk_out.shape[1]
    npts = point_index.shape[0] * n
    rows = width // n
    nz = n // 4
    row = lambda array: array.reshape(1, array.shape[0])
    vmem = pl.BlockSpec(memory_space=pltpu.VMEM)
    return pl.pallas_call(
        functools.partial(step_kernel, n),
        out_shape=(
            jax.ShapeDtypeStruct((sensors // n, width), f32),
            jax.ShapeDtypeStruct((rows, width), f32),
            jax.ShapeDtypeStruct((rows, width), f32),
        ),
        in_specs=[vmem] * 13,
        out_specs=(vmem, vmem, vmem),
        scratch_shapes=[
            pltpu.VMEM((n, point_index.shape[0], 128), f32),
            pltpu.VMEM((4 * npts, width), bf16),
            pltpu.VMEM((4 * npts, width), bf16),
            pltpu.VMEM((4, n, rows, width), bf16),
            pltpu.VMEM((4, n, rows, width), f32),
            pltpu.VMEM((4, nz, rows, width), bf16),
            pltpu.VMEM((4, nz, rows, width), f32),
            pltpu.VMEM((4, nz - 1, rows, width), bf16),
            pltpu.VMEM((4, n // 2, rows, width), bf16),
            pltpu.VMEM((4, nz, rows, width), bf16),
            pltpu.VMEM((4, nz - 1, rows, width), bf16),
            pltpu.SemaphoreType.DMA((n - 1,)),
            pltpu.SemaphoreType.DMA((n - 1,)),
            pltpu.SemaphoreType.DMA((4,)),
            pltpu.SemaphoreType.DMA((4,)),
            pltpu.SemaphoreType.DMA((4,)),
            pltpu.SemaphoreType.DMA((4,)),
            pltpu.SemaphoreType.DMA((4, nz - 1)),
            pltpu.SemaphoreType.DMA((4, nz - 1)),
        ],
        compiler_params=pltpu.CompilerParams(
            collective_id=0, has_side_effects=True, vmem_limit_bytes=48 * 2**20
        ),
    )(
        sensor_values,
        row(amplitude),
        field_modes.T,
        point_index.T,
        row(forcing),
        branch_in,
        row(branch_in_bias),
        branch_out,
        row(branch_out_bias),
        trunk_in,
        row(trunk_in_bias),
        trunk_out,
        row(trunk_out_bias),
    )


def device_step(n, *arrays):
    sensor_values, point_index, trunk_out = arrays[0], arrays[3], arrays[11]
    rows = trunk_out.shape[1] // n
    fits = (
        n % 4 == 0
        and n >= 8
        and rows % 16 == 0
        and point_index.shape[0] == 8
        and point_index.shape[0] * n == 128
        and sensor_values.shape[1] == 2 * rows * n
        and trunk_out.shape[0] == trunk_out.shape[1]
    )
    if fits:
        return fused_step(n, *arrays)
    return per_device(*arrays)


def solution(mesh):
    return jax.shard_map(
        functools.partial(device_step, mesh.shape["fn"]),
        mesh=mesh,
        in_specs=(
            P(("ens", "fn"), None),
            P(("ens", "fn")),
            P(("ens", "fn"), None),
            P(("ens", "fn"), None),
            P(("ens", "fn")),
            P(),
            P(),
            P(),
            P(),
            P(),
            P(),
            P(),
            P(),
        ),
        out_specs=(P(("ens", "fn"), None), P(("ens", "fn"), None), P(("ens", "fn"), None)),
        check_vma=False,
    )
```

```python
import functools
import math

import jax
import jax.numpy as jnp
from jax import lax
from jax.experimental import pallas as pl
from jax.experimental.pallas import tpu as pltpu
from jax.sharding import PartitionSpec as P

GRID = 128
MODES = 5
PIECE = 16
MESH = pl.DeviceIdType.MESH
ROW_DIMS = (((0,), (0,)), ((), ()))
COL_DIMS = (((1,), (1,)), ((), ()))


def grid_coords(point_index):
    return (point_index.astype(jnp.float32) + 0.5) / GRID


def trunk_hidden(coords, trunk_in, trunk_in_bias):
    pre_act = (
        coords[:, 0:1] * trunk_in[0][None, :]
        + coords[:, 1:2] * trunk_in[1][None, :]
        + trunk_in_bias[None, :]
    )
    activ = jnp.tanh(pre_act)
    first_der = 1.0 - activ * activ
    second_der = -2.0 * activ * first_der
    square_sum = trunk_in[0] * trunk_in[0] + trunk_in[1] * trunk_in[1]
    stacked = jnp.stack(
        [activ, first_der * trunk_in[0], first_der * trunk_in[1], second_der * square_sum], axis=1
    )
    return stacked.astype(jnp.bfloat16)


def trunk_tangents(hidden, trunk_out, trunk_out_bias):
    npts = hidden.shape[0]
    width = trunk_out.shape[1]
    flat_out = jnp.dot(
        hidden.reshape(npts * 4, hidden.shape[2]), trunk_out, preferred_element_type=jnp.float32
    )
    chan_mask = (jnp.arange(4) == 0).astype(jnp.float32)
    shaped = (
        flat_out.reshape(npts, 4, width) + chan_mask[None, :, None] * trunk_out_bias[None, None, :]
    )
    return shaped.astype(jnp.bfloat16)


def tile_cotangent(branch_feat, tangents, coords, forcing_pts, amplitude, field_modes):
    npts = tangents.shape[0]
    nfield = branch_feat.shape[0]
    flattened = tangents.reshape(npts * 4, tangents.shape[2])
    tile_vals = lax.dot_general(
        branch_feat, flattened, (((1,), (1,)), ((), ())), preferred_element_type=jnp.float32
    )
    tile_vals = tile_vals.reshape(nfield, npts, 4)
    x_coord = coords[:, 0][None, :]
    y_coord = coords[:, 1][None, :]
    freq_x = field_modes[:, 0:1].astype(jnp.float32) * math.pi
    freq_y = field_modes[:, 1:2].astype(jnp.float32) * math.pi
    amp_col = amplitude[:, None]
    sin_x = jnp.sin(freq_x * x_coord)
    cos_x = jnp.cos(freq_x * x_coord)
    sin_y = jnp.sin(freq_y * y_coord)
    cos_y = jnp.cos(freq_y * y_coord)
    perm = jnp.exp(amp_col * sin_x * sin_y)
    perm_dx = perm * amp_col * freq_x * cos_x * sin_y
    perm_dy = perm * amp_col * freq_y * sin_x * cos_y
    residual_tile = (
        tile_vals[:, :, 0]
        - (perm * tile_vals[:, :, 3] + perm_dx * tile_vals[:, :, 1] + perm_dy * tile_vals[:, :, 2])
        - forcing_pts.astype(jnp.float32)[None, :]
    )
    scaled = residual_tile / npts
    stacked = jnp.stack([scaled, -scaled * perm_dx, -scaled * perm_dy, -scaled * perm], axis=2)
    return stacked.astype(jnp.bfloat16).reshape(nfield, npts * 4)


def trunk_weight_grad(hidden_rows, d_tangents):
    upper_part = lax.optimization_barrier(d_tangents.astype(jnp.bfloat16))
    lower_part = (d_tangents - upper_part.astype(jnp.float32)).astype(jnp.bfloat16)
    dims = (((0,), (0,)), ((), ()))
    upper_term = lax.dot_general(hidden_rows, upper_part, dims, preferred_element_type=jnp.float32)
    lower_term = lax.dot_general(hidden_rows, lower_part, dims, preferred_element_type=jnp.float32)
    return upper_term + lower_term


def per_device(
    sensor_values,
    amplitude,
    field_modes,
    point_index,
    forcing,
    branch_in,
    branch_in_bias,
    branch_out,
    branch_out_bias,
    trunk_in,
    trunk_in_bias,
    trunk_out,
    trunk_out_bias,
):
    width = trunk_out.shape[1]
    trunk_width = trunk_out.shape[0]
    branch_hidden = jnp.tanh(
        jnp.dot(sensor_values, branch_in, preferred_element_type=jnp.float32)
        + branch_in_bias[None, :]
    ).astype(jnp.bfloat16)
    branch_feat = (
        jnp.dot(branch_hidden, branch_out, preferred_element_type=jnp.float32)
        + branch_out_bias[None, :]
    ).astype(jnp.bfloat16)
    own_coords = grid_coords(point_index)
    hidden_own = trunk_hidden(own_coords, trunk_in, trunk_in_bias)
    tangents_own = trunk_tangents(hidden_own, trunk_out, trunk_out_bias)
    tangents_all, coords_sent, forcing_all = (
        lax.all_gather(tangents_own, "fn", axis=0, tiled=True),
        lax.all_gather(own_coords.astype(jnp.bfloat16), "fn", axis=0, tiled=True),
        lax.all_gather(forcing, "fn", axis=0, tiled=True),
    )
    coords_all = coords_sent.astype(jnp.float32)
    all_points = tangents_all.shape[0]
    cotangent = tile_cotangent(
        branch_feat, tangents_all, coords_all, forcing_all, amplitude, field_modes
    )
    flattened = tangents_all.reshape(all_points * 4, width)
    d_branch = jnp.dot(cotangent, flattened, preferred_element_type=jnp.float32).astype(
        jnp.bfloat16
    )
    grad_out_part = lax.dot_general(
        branch_hidden, d_branch, (((0,), (0,)), ((), ())), preferred_element_type=jnp.float32
    )
    hidden_f = branch_hidden.astype(jnp.float32)
    d_pre = (
        lax.dot_general(
            d_branch, branch_out, (((1,), (1,)), ((), ())), preferred_element_type=jnp.float32
        )
        * (1.0 - hidden_f * hidden_f)
    ).astype(jnp.bfloat16)
    grad_in_part = lax.dot_general(
        sensor_values, d_pre, (((0,), (0,)), ((), ())), preferred_element_type=jnp.float32
    )
    own_rows = hidden_own.shape[0] * 4
    d_tangents = lax.psum_scatter(
        lax.dot_general(
            cotangent, branch_feat, (((0,), (0,)), ((), ())), preferred_element_type=jnp.float32
        ),
        "fn",
        scatter_dimension=0,
        tiled=True,
    )
    hidden_rows = hidden_own.reshape(own_rows, trunk_width)
    grad_trunk_part = trunk_weight_grad(hidden_rows, d_tangents)
    grad_branch_in, grad_branch_out, grad_trunk_out = (
        lax.psum_scatter(grad_in_part, "fn", scatter_dimension=0, tiled=True),
        lax.psum_scatter(grad_out_part, "fn", scatter_dimension=0, tiled=True),
        lax.psum_scatter(grad_trunk_part, "fn", scatter_dimension=0, tiled=True),
    )
    return (grad_branch_in, grad_branch_out, grad_trunk_out)


def to_column(row, count):
    rows = lax.broadcasted_iota(jnp.int32, (count, count), 0)
    lanes = lax.broadcasted_iota(jnp.int32, (count, count), 1)
    return jnp.sum(jnp.where(rows == lanes, row, 0.0), axis=1, keepdims=True)


def spread_rows(row, lanes):
    return jnp.broadcast_to(row, (lanes, row.shape[1])).T


def pick_mode(modes, table):
    picked = jnp.broadcast_to(table[0:1, :], modes.shape)
    for mode in range(2, MODES + 1):
        picked = jnp.where(modes == float(mode), table[mode - 1 : mode, :], picked)
    return picked


def step_kernel(n, *refs):
    hbm, refs = refs[:13], refs[13:]
    out_ref, refs = refs[0], refs[1:]
    staged, refs = refs[:13], refs[13:]
    (
        sensors,
        amplitude,
        modes,
        points,
        forcing,
        branch_in,
        branch_in_bias,
        branch_out,
        branch_out_bias,
        trunk_in,
        trunk_in_bias,
        trunk_out,
        trunk_out_bias,
    ) = staged
    (
        pts,
        hid,
        tang,
        part,
        wide,
        half_send,
        half_keep,
        quarter_send,
        from_core,
        from_y,
        from_z,
        load_sem,
        pts_send,
        pts_recv,
        core_send,
        core_recv,
        y_send,
        y_recv,
        z_send,
        z_recv,
    ) = refs
    f32, bf16 = jnp.float32, jnp.bfloat16
    me = lax.axis_index("fn")
    nz = n // 4
    core = lax.rem(me, 2)
    y_at = lax.rem(me // 2, 2)
    z_at = me // 4
    other_core = me + 1 - 2 * core
    other_y = me + 2 - 4 * y_at
    own = points.shape[1]
    npts = own * n
    rows = from_z.shape[2]
    out_rows = out_ref.shape[0] // 4

    barrier = pltpu.get_barrier_semaphore()
    for k in range(1, n):
        pl.semaphore_signal(
            barrier, inc=1, device_id={"fn": lax.rem(me + k, n)}, device_id_type=MESH
        )

    loads = [pltpu.make_async_copy(hbm[i], staged[i], load_sem.at[i]) for i in range(13)]
    for i in (3, 4, 0, 5, 6, 7, 8, 1, 2, 9, 10, 11, 12):
        loads[i].start()

    loads[3].wait()
    loads[4].wait()
    coords = (points[...].astype(f32) + 0.5) / GRID
    lane = lax.broadcasted_iota(jnp.int32, (own, 128), 1)
    pts[me] = jnp.where(
        lane == 0,
        to_column(coords[0:1, :], own),
        jnp.where(
            lane == 1,
            to_column(coords[1:2, :], own),
            to_column(forcing[...].astype(f32), own),
        ),
    )
    pl.semaphore_wait(barrier, n - 1)

    def points_copy(k):
        return pltpu.make_async_remote_copy(
            src_ref=pts.at[me],
            dst_ref=pts.at[me],
            send_sem=pts_send.at[k - 1],
            recv_sem=pts_recv.at[k - 1],
            device_id={"fn": lax.rem(me + k, n)},
            device_id_type=MESH,
        )

    def points_arrival(k):
        source = lax.rem(me + n - k, n)
        return pltpu.make_async_remote_copy(
            src_ref=pts.at[source],
            dst_ref=pts.at[source],
            send_sem=pts_send.at[k - 1],
            recv_sem=pts_recv.at[k - 1],
            device_id={"fn": source},
            device_id_type=MESH,
        )

    for k in far_first(n):
        points_copy(k).start()

    for i in (0, 5, 6):
        loads[i].wait()
    hidden = jnp.tanh(
        jnp.dot(sensors[...], branch_in[...], preferred_element_type=f32) + branch_in_bias[...]
    ).astype(bf16)

    for i in (7, 8, 1, 2):
        loads[i].wait()
    feat = (
        jnp.dot(hidden, branch_out[...], preferred_element_type=f32) + branch_out_bias[...]
    ).astype(bf16)
    fields = feat.shape[0]
    amp = spread_rows(amplitude[...], npts)
    mode_x = spread_rows(modes[0:1, :].astype(f32), npts)
    mode_y = spread_rows(modes[1:2, :].astype(f32), npts)

    for i in (9, 10, 11, 12):
        loads[i].wait()
    for k in range(1, n):
        points_arrival(k).wait_recv()
    columns = pts[...].reshape(npts, 128)
    lines = columns.T
    x_row, y_row, force_row = lines[0:1, :], lines[1:2, :], lines[2:3, :]

    weight_x, weight_y = trunk_in[0:1, :], trunk_in[1:2, :]
    act = jnp.tanh(columns[:, 0:1] * weight_x + columns[:, 1:2] * weight_y + trunk_in_bias[...])
    first = 1.0 - act * act
    second = -2.0 * act * first
    hid[0:npts, :] = act.astype(bf16)
    hid[npts : 2 * npts, :] = (first * weight_x).astype(bf16)
    hid[2 * npts : 3 * npts, :] = (first * weight_y).astype(bf16)
    hid[3 * npts : 4 * npts, :] = (
        second * (weight_x * weight_x + weight_y * weight_y)
    ).astype(bf16)
    flat = jnp.dot(hid[...], trunk_out[...], preferred_element_type=f32)
    tang[0:npts, :] = (flat[0:npts, :] + trunk_out_bias[...]).astype(bf16)
    tang[npts:, :] = flat[npts:, :].astype(bf16)

    tile = lax.dot_general(feat, tang[...], COL_DIMS, preferred_element_type=f32)

    freqs = (lax.broadcasted_iota(jnp.int32, (8, npts), 0) + 1).astype(f32) * math.pi
    sin_x = pick_mode(mode_x, jnp.sin(freqs * x_row))
    cos_x = pick_mode(mode_x, jnp.cos(freqs * x_row))
    sin_y = pick_mode(mode_y, jnp.sin(freqs * y_row))
    cos_y = pick_mode(mode_y, jnp.cos(freqs * y_row))
    perm = jnp.exp(amp * sin_x * sin_y)
    perm_dx = perm * amp * (mode_x * math.pi) * cos_x * sin_y
    perm_dy = perm * amp * (mode_y * math.pi) * sin_x * cos_y
    residual = (
        tile[:, 0:npts]
        - (
            perm * tile[:, 3 * npts :]
            + perm_dx * tile[:, npts : 2 * npts]
            + perm_dy * tile[:, 2 * npts : 3 * npts]
        )
        - force_row
    )
    scaled = residual / npts
    cot = jnp.concatenate(
        [
            scaled.astype(bf16),
            (-scaled * perm_dx).astype(bf16),
            (-scaled * perm_dy).astype(bf16),
            (-scaled * perm).astype(bf16),
        ],
        axis=1,
    )

    def keep(piece, value, chunk, start):
        for d in range(n):
            at = (d % 2) * (n // 2) + ((d // 2) % 2) * nz + d // 4
            block = value[d * chunk + start : d * chunk + start + rows, :]
            wide[piece, at] = block
            part[piece, at] = block.astype(bf16)

    def core_copy(piece):
        return pltpu.make_async_remote_copy(
            src_ref=part.at[piece, pl.ds((1 - core) * (n // 2), n // 2)],
            dst_ref=from_core.at[piece],
            send_sem=core_send.at[piece],
            recv_sem=core_recv.at[piece],
            device_id={"fn": other_core},
            device_id_type=MESH,
        )

    def y_copy(piece):
        return pltpu.make_async_remote_copy(
            src_ref=half_send.at[piece],
            dst_ref=from_y.at[piece],
            send_sem=y_send.at[piece],
            recv_sem=y_recv.at[piece],
            device_id={"fn": other_y},
            device_id_type=MESH,
        )

    def z_copy(piece, k):
        return pltpu.make_async_remote_copy(
            src_ref=quarter_send.at[piece, k - 1],
            dst_ref=from_z.at[piece, k - 1],
            send_sem=z_send.at[piece, k - 1],
            recv_sem=z_recv.at[piece, k - 1],
            device_id={"fn": lax.rem(me + 4 * k, n)},
            device_id_type=MESH,
        )

    def core_to_y(piece):
        core_copy(piece).wait_recv()
        away = (1 - y_at) * nz
        half_send[piece] = (
            wide[piece, pl.ds(core * (n // 2) + away, nz)]
            + from_core[piece, pl.ds(away, nz)].astype(f32)
        ).astype(bf16)
        y_copy(piece).start()
        half_keep[piece] = wide[piece, pl.ds(core * (n // 2) + y_at * nz, nz)] + from_core[
            piece, pl.ds(y_at * nz, nz)
        ].astype(f32)

    def y_to_z(piece):
        y_copy(piece).wait_recv()
        for k in range(1, nz):
            target = lax.rem(z_at + k, nz)
            quarter_send[piece, k - 1] = (
                half_keep[piece, target] + from_y[piece, target].astype(f32)
            ).astype(bf16)
            z_copy(piece, k).start()

    def finish(piece):
        total = half_keep[piece, z_at] + from_y[piece, z_at].astype(f32)
        for k in range(1, nz):
            z_copy(piece, k).wait_recv()
            total = total + from_z[piece, k - 1].astype(f32)
        return total

    unit = out_rows // rows
    d_branch = jnp.dot(cot, tang[...], preferred_element_type=f32).astype(bf16)
    grad_out = lax.dot_general(hidden, d_branch, ROW_DIMS, preferred_element_type=f32)
    for i in range(unit):
        keep(i, grad_out, out_rows, i * rows)
        core_copy(i).start()

    hidden_f = hidden.astype(f32)
    d_pre = (
        lax.dot_general(d_branch, branch_out[...], COL_DIMS, preferred_element_type=f32)
        * (1.0 - hidden_f * hidden_f)
    ).astype(bf16)
    for i in range(unit):
        core_to_y(i)
    grad_in = lax.dot_general(sensors[...], d_pre, ROW_DIMS, preferred_element_type=f32)
    for i in range(2 * unit):
        keep(unit + i, grad_in, 2 * out_rows, i * rows)
        core_copy(unit + i).start()

    trunk_mix = jnp.dot(cot, hid[...], preferred_element_type=f32)
    upper = trunk_mix.astype(bf16)
    lower = (trunk_mix - upper.astype(f32)).astype(bf16)
    for i in range(unit):
        core_to_y(unit + i)
    grad_trunk = lax.dot_general(
        upper, feat, ROW_DIMS, preferred_element_type=f32
    ) + lax.dot_general(lower, feat, ROW_DIMS, preferred_element_type=f32)
    for i in range(unit):
        keep(3 * unit + i, grad_trunk, out_rows, i * rows)
        core_copy(3 * unit + i).start()
    y_to_z(0)
    for i in range(2 * unit, 4 * unit):
        core_to_y(i)
        y_to_z(i - 2 * unit + 1)
    for i in range(2 * unit + 1, 4 * unit):
        y_to_z(i)
    for i in range(4 * unit):
        out_ref[i * rows : (i + 1) * rows, :] = finish(i)

    for k in range(1, n):
        points_copy(k).wait_send()
    for piece in range(4 * unit):
        core_copy(piece).wait_send()
        y_copy(piece).wait_send()
        for k in range(1, nz):
            z_copy(piece, k).wait_send()


def far_first(n):
    return sorted(range(1, n), key=lambda k: -min(k, n - k))


def split_kernel(sums, grad_in, grad_out, grad_trunk, sems):
    rows = grad_out.shape[0]
    moves = [
        pltpu.make_async_copy(sums.at[pl.ds(start, out.shape[0])], out, sems.at[i])
        for i, (start, out) in enumerate(
            ((rows, grad_in), (0, grad_out), (3 * rows, grad_trunk))
        )
    ]
    for move in moves:
        move.start()
    for move in moves:
        move.wait()


def fused_step(
    n,
    sensor_values,
    amplitude,
    field_modes,
    point_index,
    forcing,
    branch_in,
    branch_in_bias,
    branch_out,
    branch_out_bias,
    trunk_in,
    trunk_in_bias,
    trunk_out,
    trunk_out_bias,
):
    f32, bf16 = jnp.float32, jnp.bfloat16
    width = trunk_out.shape[1]
    own = point_index.shape[0]
    npts = own * n
    out_rows = width // n
    rows = PIECE
    pieces = 4 * out_rows // rows
    nz = n // 4
    row = lambda array: array.reshape(1, array.shape[0])
    operands = (
        sensor_values,
        row(amplitude),
        field_modes.T,
        point_index.T,
        row(forcing),
        branch_in,
        row(branch_in_bias),
        branch_out,
        row(branch_out_bias),
        trunk_in,
        row(trunk_in_bias),
        trunk_out,
        row(trunk_out_bias),
    )
    hbm = pl.BlockSpec(memory_space=pl.ANY)
    vmem = pl.BlockSpec(memory_space=pltpu.VMEM)
    sums = pl.pallas_call(
        functools.partial(step_kernel, n),
        out_shape=jax.ShapeDtypeStruct((4 * out_rows, width), f32),
        in_specs=[pl.BlockSpec(memory_space=pltpu.HBM)] * len(operands),
        out_specs=vmem,
        scratch_shapes=[pltpu.VMEM(array.shape, array.dtype) for array in operands]
        + [
            pltpu.VMEM((n, own, 128), f32),
            pltpu.VMEM((4 * npts, width), bf16),
            pltpu.VMEM((4 * npts, width), bf16),
            pltpu.VMEM((pieces, n, rows, width), bf16),
            pltpu.VMEM((pieces, n, rows, width), f32),
            pltpu.VMEM((pieces, nz, rows, width), bf16),
            pltpu.VMEM((pieces, nz, rows, width), f32),
            pltpu.VMEM((pieces, nz - 1, rows, width), bf16),
            pltpu.VMEM((pieces, n // 2, rows, width), bf16),
            pltpu.VMEM((pieces, nz, rows, width), bf16),
            pltpu.VMEM((pieces, nz - 1, rows, width), bf16),
            pltpu.SemaphoreType.DMA((len(operands),)),
            pltpu.SemaphoreType.DMA((n - 1,)),
            pltpu.SemaphoreType.DMA((n - 1,)),
            pltpu.SemaphoreType.DMA((pieces,)),
            pltpu.SemaphoreType.DMA((pieces,)),
            pltpu.SemaphoreType.DMA((pieces,)),
            pltpu.SemaphoreType.DMA((pieces,)),
            pltpu.SemaphoreType.DMA((pieces, nz - 1)),
            pltpu.SemaphoreType.DMA((pieces, nz - 1)),
        ],
        compiler_params=pltpu.CompilerParams(
            collective_id=0, has_side_effects=True, vmem_limit_bytes=60 * 2**20
        ),
    )(*operands)
    return pl.pallas_call(
        split_kernel,
        out_shape=(
            jax.ShapeDtypeStruct((2 * out_rows, width), f32),
            jax.ShapeDtypeStruct((out_rows, width), f32),
            jax.ShapeDtypeStruct((out_rows, width), f32),
        ),
        in_specs=[vmem],
        out_specs=(hbm, hbm, hbm),
        scratch_shapes=[pltpu.SemaphoreType.DMA((3,))],
    )(sums)


def device_step(n, *arrays):
    sensor_values, point_index, trunk_out = arrays[0], arrays[3], arrays[11]
    rows = trunk_out.shape[1] // n
    fits = (
        n % 4 == 0
        and n >= 8
        and rows % 16 == 0
        and point_index.shape[0] == 8
        and point_index.shape[0] * n == 128
        and sensor_values.shape[1] == 2 * rows * n
        and trunk_out.shape[0] == trunk_out.shape[1]
    )
    if fits:
        return fused_step(n, *arrays)
    return per_device(*arrays)


def solution(mesh):
    return jax.shard_map(
        functools.partial(device_step, mesh.shape["fn"]),
        mesh=mesh,
        in_specs=(
            P(("ens", "fn"), None),
            P(("ens", "fn")),
            P(("ens", "fn"), None),
            P(("ens", "fn"), None),
            P(("ens", "fn")),
            P(),
            P(),
            P(),
            P(),
            P(),
            P(),
            P(),
            P(),
        ),
        out_specs=(P(("ens", "fn"), None), P(("ens", "fn"), None), P(("ens", "fn"), None)),
        check_vma=False,
    )
```

```python
import functools
import math

import jax
import jax.numpy as jnp
from jax import lax
from jax.experimental import pallas as pl
from jax.experimental.pallas import tpu as pltpu
from jax.sharding import PartitionSpec as P

GRID = 128
MODES = 5
PIECE = 16
Z_FIRST = (1, 2)
MESH = pl.DeviceIdType.MESH
ROW_DIMS = (((0,), (0,)), ((), ()))
COL_DIMS = (((1,), (1,)), ((), ()))


def grid_coords(point_index):
    return (point_index.astype(jnp.float32) + 0.5) / GRID


def trunk_hidden(coords, trunk_in, trunk_in_bias):
    pre_act = (
        coords[:, 0:1] * trunk_in[0][None, :]
        + coords[:, 1:2] * trunk_in[1][None, :]
        + trunk_in_bias[None, :]
    )
    activ = jnp.tanh(pre_act)
    first_der = 1.0 - activ * activ
    second_der = -2.0 * activ * first_der
    square_sum = trunk_in[0] * trunk_in[0] + trunk_in[1] * trunk_in[1]
    stacked = jnp.stack(
        [activ, first_der * trunk_in[0], first_der * trunk_in[1], second_der * square_sum], axis=1
    )
    return stacked.astype(jnp.bfloat16)


def trunk_tangents(hidden, trunk_out, trunk_out_bias):
    npts = hidden.shape[0]
    width = trunk_out.shape[1]
    flat_out = jnp.dot(
        hidden.reshape(npts * 4, hidden.shape[2]), trunk_out, preferred_element_type=jnp.float32
    )
    chan_mask = (jnp.arange(4) == 0).astype(jnp.float32)
    shaped = (
        flat_out.reshape(npts, 4, width) + chan_mask[None, :, None] * trunk_out_bias[None, None, :]
    )
    return shaped.astype(jnp.bfloat16)


def tile_cotangent(branch_feat, tangents, coords, forcing_pts, amplitude, field_modes):
    npts = tangents.shape[0]
    nfield = branch_feat.shape[0]
    flattened = tangents.reshape(npts * 4, tangents.shape[2])
    tile_vals = lax.dot_general(
        branch_feat, flattened, (((1,), (1,)), ((), ())), preferred_element_type=jnp.float32
    )
    tile_vals = tile_vals.reshape(nfield, npts, 4)
    x_coord = coords[:, 0][None, :]
    y_coord = coords[:, 1][None, :]
    freq_x = field_modes[:, 0:1].astype(jnp.float32) * math.pi
    freq_y = field_modes[:, 1:2].astype(jnp.float32) * math.pi
    amp_col = amplitude[:, None]
    sin_x = jnp.sin(freq_x * x_coord)
    cos_x = jnp.cos(freq_x * x_coord)
    sin_y = jnp.sin(freq_y * y_coord)
    cos_y = jnp.cos(freq_y * y_coord)
    perm = jnp.exp(amp_col * sin_x * sin_y)
    perm_dx = perm * amp_col * freq_x * cos_x * sin_y
    perm_dy = perm * amp_col * freq_y * sin_x * cos_y
    residual_tile = (
        tile_vals[:, :, 0]
        - (perm * tile_vals[:, :, 3] + perm_dx * tile_vals[:, :, 1] + perm_dy * tile_vals[:, :, 2])
        - forcing_pts.astype(jnp.float32)[None, :]
    )
    scaled = residual_tile / npts
    stacked = jnp.stack([scaled, -scaled * perm_dx, -scaled * perm_dy, -scaled * perm], axis=2)
    return stacked.astype(jnp.bfloat16).reshape(nfield, npts * 4)


def trunk_weight_grad(hidden_rows, d_tangents):
    upper_part = lax.optimization_barrier(d_tangents.astype(jnp.bfloat16))
    lower_part = (d_tangents - upper_part.astype(jnp.float32)).astype(jnp.bfloat16)
    dims = (((0,), (0,)), ((), ()))
    upper_term = lax.dot_general(hidden_rows, upper_part, dims, preferred_element_type=jnp.float32)
    lower_term = lax.dot_general(hidden_rows, lower_part, dims, preferred_element_type=jnp.float32)
    return upper_term + lower_term


def per_device(
    sensor_values,
    amplitude,
    field_modes,
    point_index,
    forcing,
    branch_in,
    branch_in_bias,
    branch_out,
    branch_out_bias,
    trunk_in,
    trunk_in_bias,
    trunk_out,
    trunk_out_bias,
):
    width = trunk_out.shape[1]
    trunk_width = trunk_out.shape[0]
    branch_hidden = jnp.tanh(
        jnp.dot(sensor_values, branch_in, preferred_element_type=jnp.float32)
        + branch_in_bias[None, :]
    ).astype(jnp.bfloat16)
    branch_feat = (
        jnp.dot(branch_hidden, branch_out, preferred_element_type=jnp.float32)
        + branch_out_bias[None, :]
    ).astype(jnp.bfloat16)
    own_coords = grid_coords(point_index)
    hidden_own = trunk_hidden(own_coords, trunk_in, trunk_in_bias)
    tangents_own = trunk_tangents(hidden_own, trunk_out, trunk_out_bias)
    tangents_all, coords_sent, forcing_all = (
        lax.all_gather(tangents_own, "fn", axis=0, tiled=True),
        lax.all_gather(own_coords.astype(jnp.bfloat16), "fn", axis=0, tiled=True),
        lax.all_gather(forcing, "fn", axis=0, tiled=True),
    )
    coords_all = coords_sent.astype(jnp.float32)
    all_points = tangents_all.shape[0]
    cotangent = tile_cotangent(
        branch_feat, tangents_all, coords_all, forcing_all, amplitude, field_modes
    )
    flattened = tangents_all.reshape(all_points * 4, width)
    d_branch = jnp.dot(cotangent, flattened, preferred_element_type=jnp.float32).astype(
        jnp.bfloat16
    )
    grad_out_part = lax.dot_general(
        branch_hidden, d_branch, (((0,), (0,)), ((), ())), preferred_element_type=jnp.float32
    )
    hidden_f = branch_hidden.astype(jnp.float32)
    d_pre = (
        lax.dot_general(
            d_branch, branch_out, (((1,), (1,)), ((), ())), preferred_element_type=jnp.float32
        )
        * (1.0 - hidden_f * hidden_f)
    ).astype(jnp.bfloat16)
    grad_in_part = lax.dot_general(
        sensor_values, d_pre, (((0,), (0,)), ((), ())), preferred_element_type=jnp.float32
    )
    own_rows = hidden_own.shape[0] * 4
    d_tangents = lax.psum_scatter(
        lax.dot_general(
            cotangent, branch_feat, (((0,), (0,)), ((), ())), preferred_element_type=jnp.float32
        ),
        "fn",
        scatter_dimension=0,
        tiled=True,
    )
    hidden_rows = hidden_own.reshape(own_rows, trunk_width)
    grad_trunk_part = trunk_weight_grad(hidden_rows, d_tangents)
    grad_branch_in, grad_branch_out, grad_trunk_out = (
        lax.psum_scatter(grad_in_part, "fn", scatter_dimension=0, tiled=True),
        lax.psum_scatter(grad_out_part, "fn", scatter_dimension=0, tiled=True),
        lax.psum_scatter(grad_trunk_part, "fn", scatter_dimension=0, tiled=True),
    )
    return (grad_branch_in, grad_branch_out, grad_trunk_out)


def to_column(row, count):
    rows = lax.broadcasted_iota(jnp.int32, (count, count), 0)
    lanes = lax.broadcasted_iota(jnp.int32, (count, count), 1)
    return jnp.sum(jnp.where(rows == lanes, row, 0.0), axis=1, keepdims=True)


def spread_rows(row, lanes):
    return jnp.broadcast_to(row, (lanes, row.shape[1])).T


def pick_mode(modes, table):
    picked = jnp.broadcast_to(table[0:1, :], modes.shape)
    for mode in range(2, MODES + 1):
        picked = jnp.where(modes == float(mode), table[mode - 1 : mode, :], picked)
    return picked


def step_kernel(n, *refs):
    hbm, refs = refs[:13], refs[13:]
    out_ref, refs = refs[0], refs[1:]
    staged, refs = refs[:13], refs[13:]
    (
        sensors,
        amplitude,
        modes,
        points,
        forcing,
        branch_in,
        branch_in_bias,
        branch_out,
        branch_out_bias,
        trunk_in,
        trunk_in_bias,
        trunk_out,
        trunk_out_bias,
    ) = staged
    (
        pts,
        hid,
        tang,
        part,
        wide,
        half_send,
        half_keep,
        quarter_send,
        from_core,
        from_y,
        from_z,
        lines_send,
        from_lines,
        last_send,
        from_last,
        load_sem,
        pts_send,
        pts_recv,
        core_send,
        core_recv,
        y_send,
        y_recv,
        z_send,
        z_recv,
    ) = refs
    f32, bf16 = jnp.float32, jnp.bfloat16
    me = lax.axis_index("fn")
    nz = n // 4
    core = lax.rem(me, 2)
    y_at = lax.rem(me // 2, 2)
    z_at = me // 4
    other_core = me + 1 - 2 * core
    other_y = me + 2 - 4 * y_at
    own = points.shape[1]
    npts = own * n
    rows = from_z.shape[2]
    out_rows = out_ref.shape[0] // 4

    barrier = pltpu.get_barrier_semaphore()
    for k in range(1, n):
        pl.semaphore_signal(
            barrier, inc=1, device_id={"fn": lax.rem(me + k, n)}, device_id_type=MESH
        )

    loads = [pltpu.make_async_copy(hbm[i], staged[i], load_sem.at[i]) for i in range(13)]
    for i in (3, 4, 0, 5, 6, 7, 8, 1, 2, 9, 10, 11, 12):
        loads[i].start()

    loads[3].wait()
    loads[4].wait()
    coords = (points[...].astype(f32) + 0.5) / GRID
    lane = lax.broadcasted_iota(jnp.int32, (own, 128), 1)
    pts[me] = jnp.where(
        lane == 0,
        to_column(coords[0:1, :], own),
        jnp.where(
            lane == 1,
            to_column(coords[1:2, :], own),
            to_column(forcing[...].astype(f32), own),
        ),
    )
    pl.semaphore_wait(barrier, n - 1)

    def points_copy(k):
        return pltpu.make_async_remote_copy(
            src_ref=pts.at[me],
            dst_ref=pts.at[me],
            send_sem=pts_send.at[k - 1],
            recv_sem=pts_recv.at[k - 1],
            device_id={"fn": lax.rem(me + k, n)},
            device_id_type=MESH,
        )

    def points_arrival(k):
        source = lax.rem(me + n - k, n)
        return pltpu.make_async_remote_copy(
            src_ref=pts.at[source],
            dst_ref=pts.at[source],
            send_sem=pts_send.at[k - 1],
            recv_sem=pts_recv.at[k - 1],
            device_id={"fn": source},
            device_id_type=MESH,
        )

    for k in far_first(n):
        points_copy(k).start()

    for i in (0, 5, 6):
        loads[i].wait()
    hidden = jnp.tanh(
        jnp.dot(sensors[...], branch_in[...], preferred_element_type=f32) + branch_in_bias[...]
    ).astype(bf16)

    for i in (7, 8, 1, 2):
        loads[i].wait()
    feat = (
        jnp.dot(hidden, branch_out[...], preferred_element_type=f32) + branch_out_bias[...]
    ).astype(bf16)
    fields = feat.shape[0]
    amp = spread_rows(amplitude[...], npts)
    mode_x = spread_rows(modes[0:1, :].astype(f32), npts)
    mode_y = spread_rows(modes[1:2, :].astype(f32), npts)

    for i in (9, 10, 11, 12):
        loads[i].wait()
    for k in range(1, n):
        points_arrival(k).wait_recv()
    columns = pts[...].reshape(npts, 128)
    lines = columns.T
    x_row, y_row, force_row = lines[0:1, :], lines[1:2, :], lines[2:3, :]

    weight_x, weight_y = trunk_in[0:1, :], trunk_in[1:2, :]
    act = jnp.tanh(columns[:, 0:1] * weight_x + columns[:, 1:2] * weight_y + trunk_in_bias[...])
    first = 1.0 - act * act
    second = -2.0 * act * first
    hid[0:npts, :] = act.astype(bf16)
    hid[npts : 2 * npts, :] = (first * weight_x).astype(bf16)
    hid[2 * npts : 3 * npts, :] = (first * weight_y).astype(bf16)
    hid[3 * npts : 4 * npts, :] = (
        second * (weight_x * weight_x + weight_y * weight_y)
    ).astype(bf16)
    flat = jnp.dot(hid[...], trunk_out[...], preferred_element_type=f32)
    tang[0:npts, :] = (flat[0:npts, :] + trunk_out_bias[...]).astype(bf16)
    tang[npts:, :] = flat[npts:, :].astype(bf16)

    tile = lax.dot_general(feat, tang[...], COL_DIMS, preferred_element_type=f32)

    freqs = (lax.broadcasted_iota(jnp.int32, (8, npts), 0) + 1).astype(f32) * math.pi
    sin_x = pick_mode(mode_x, jnp.sin(freqs * x_row))
    cos_x = pick_mode(mode_x, jnp.cos(freqs * x_row))
    sin_y = pick_mode(mode_y, jnp.sin(freqs * y_row))
    cos_y = pick_mode(mode_y, jnp.cos(freqs * y_row))
    perm = jnp.exp(amp * sin_x * sin_y)
    perm_dx = perm * amp * (mode_x * math.pi) * cos_x * sin_y
    perm_dy = perm * amp * (mode_y * math.pi) * sin_x * cos_y
    residual = (
        tile[:, 0:npts]
        - (
            perm * tile[:, 3 * npts :]
            + perm_dx * tile[:, npts : 2 * npts]
            + perm_dy * tile[:, 2 * npts : 3 * npts]
        )
        - force_row
    )
    scaled = residual / npts
    cot = jnp.concatenate(
        [
            scaled.astype(bf16),
            (-scaled * perm_dx).astype(bf16),
            (-scaled * perm_dy).astype(bf16),
            (-scaled * perm).astype(bf16),
        ],
        axis=1,
    )

    def keep(piece, value, chunk, start):
        for d in range(n):
            at = (d % 2) * (n // 2) + ((d // 2) % 2) * nz + d // 4
            block = value[d * chunk + start : d * chunk + start + rows, :]
            wide[piece, at] = block
            part[piece, at] = block.astype(bf16)

    def core_copy(piece):
        return pltpu.make_async_remote_copy(
            src_ref=part.at[piece, pl.ds((1 - core) * (n // 2), n // 2)],
            dst_ref=from_core.at[piece],
            send_sem=core_send.at[piece],
            recv_sem=core_recv.at[piece],
            device_id={"fn": other_core},
            device_id_type=MESH,
        )

    def y_copy(piece):
        return pltpu.make_async_remote_copy(
            src_ref=half_send.at[piece],
            dst_ref=from_y.at[piece],
            send_sem=y_send.at[piece],
            recv_sem=y_recv.at[piece],
            device_id={"fn": other_y},
            device_id_type=MESH,
        )

    def z_copy(piece, k):
        return pltpu.make_async_remote_copy(
            src_ref=quarter_send.at[piece, k - 1],
            dst_ref=from_z.at[piece, k - 1],
            send_sem=z_send.at[piece, k - 1],
            recv_sem=z_recv.at[piece, k - 1],
            device_id={"fn": lax.rem(me + 4 * k, n)},
            device_id_type=MESH,
        )

    def line_copy(piece, k):
        slot = Z_FIRST.index(piece)
        return pltpu.make_async_remote_copy(
            src_ref=lines_send.at[slot, k - 1],
            dst_ref=from_lines.at[slot, k - 1],
            send_sem=z_send.at[piece, k - 1],
            recv_sem=z_recv.at[piece, k - 1],
            device_id={"fn": lax.rem(me + 4 * k, n)},
            device_id_type=MESH,
        )

    def last_copy(piece):
        slot = Z_FIRST.index(piece)
        return pltpu.make_async_remote_copy(
            src_ref=last_send.at[slot],
            dst_ref=from_last.at[slot],
            send_sem=y_send.at[piece],
            recv_sem=y_recv.at[piece],
            device_id={"fn": other_y},
            device_id_type=MESH,
        )

    def core_sum(piece, y, z):
        return wide[piece, core * (n // 2) + y * nz + z] + from_core[piece, y * nz + z].astype(
            f32
        )

    def core_to_lines(piece):
        core_copy(piece).wait_recv()
        for k in range(1, nz):
            target = lax.rem(z_at + k, nz)
            for y in range(2):
                lines_send[Z_FIRST.index(piece), k - 1, y] = core_sum(piece, y, target).astype(
                    bf16
                )
            line_copy(piece, k).start()

    def lines_to_y(piece):
        slot = Z_FIRST.index(piece)
        away, own_sum = core_sum(piece, 1 - y_at, z_at), core_sum(piece, y_at, z_at)
        for k in range(1, nz):
            line_copy(piece, k).wait_recv()
            away = away + from_lines[slot, k - 1, 1 - y_at].astype(f32)
            own_sum = own_sum + from_lines[slot, k - 1, y_at].astype(f32)
        last_send[slot] = away.astype(bf16)
        last_copy(piece).start()
        half_keep[piece, 0] = own_sum

    def core_to_y(piece):
        if piece in Z_FIRST:
            core_to_lines(piece)
            return
        core_copy(piece).wait_recv()
        away = (1 - y_at) * nz
        half_send[piece] = (
            wide[piece, pl.ds(core * (n // 2) + away, nz)]
            + from_core[piece, pl.ds(away, nz)].astype(f32)
        ).astype(bf16)
        y_copy(piece).start()
        half_keep[piece] = wide[piece, pl.ds(core * (n // 2) + y_at * nz, nz)] + from_core[
            piece, pl.ds(y_at * nz, nz)
        ].astype(f32)

    def y_to_z(piece):
        if piece in Z_FIRST:
            return
        y_copy(piece).wait_recv()
        for k in range(1, nz):
            target = lax.rem(z_at + k, nz)
            quarter_send[piece, k - 1] = (
                half_keep[piece, target] + from_y[piece, target].astype(f32)
            ).astype(bf16)
            z_copy(piece, k).start()

    def finish(piece):
        if piece in Z_FIRST:
            last_copy(piece).wait_recv()
            return half_keep[piece, 0] + from_last[Z_FIRST.index(piece)].astype(f32)
        total = half_keep[piece, z_at] + from_y[piece, z_at].astype(f32)
        for k in range(1, nz):
            z_copy(piece, k).wait_recv()
            total = total + from_z[piece, k - 1].astype(f32)
        return total

    unit = out_rows // rows
    d_branch = jnp.dot(cot, tang[...], preferred_element_type=f32).astype(bf16)
    grad_out = lax.dot_general(hidden, d_branch, ROW_DIMS, preferred_element_type=f32)
    for i in range(unit):
        keep(i, grad_out, out_rows, i * rows)
        core_copy(i).start()

    hidden_f = hidden.astype(f32)
    d_pre = (
        lax.dot_general(d_branch, branch_out[...], COL_DIMS, preferred_element_type=f32)
        * (1.0 - hidden_f * hidden_f)
    ).astype(bf16)
    for i in range(unit):
        core_to_y(i)
    grad_in = lax.dot_general(sensors[...], d_pre, ROW_DIMS, preferred_element_type=f32)
    for i in range(2 * unit):
        keep(unit + i, grad_in, 2 * out_rows, i * rows)
        core_copy(unit + i).start()

    trunk_mix = jnp.dot(cot, hid[...], preferred_element_type=f32)
    upper = trunk_mix.astype(bf16)
    lower = (trunk_mix - upper.astype(f32)).astype(bf16)
    for i in range(unit):
        core_to_y(unit + i)
    grad_trunk = lax.dot_general(
        upper, feat, ROW_DIMS, preferred_element_type=f32
    ) + lax.dot_general(lower, feat, ROW_DIMS, preferred_element_type=f32)
    for i in range(unit):
        keep(3 * unit + i, grad_trunk, out_rows, i * rows)
        core_copy(3 * unit + i).start()
    y_to_z(0)
    for i in range(2 * unit, 4 * unit):
        core_to_y(i)
        y_to_z(i - 2 * unit + 1)
    for piece in Z_FIRST:
        lines_to_y(piece)
    for i in range(2 * unit + 1, 4 * unit):
        y_to_z(i)
    for i in range(4 * unit):
        out_ref[i * rows : (i + 1) * rows, :] = finish(i)

    for k in range(1, n):
        points_copy(k).wait_send()
    for piece in range(4 * unit):
        core_copy(piece).wait_send()
        (last_copy if piece in Z_FIRST else y_copy)(piece).wait_send()
        for k in range(1, nz):
            (line_copy if piece in Z_FIRST else z_copy)(piece, k).wait_send()


def far_first(n):
    return sorted(range(1, n), key=lambda k: -min(k, n - k))


def split_kernel(sums, grad_in, grad_out, grad_trunk, sems):
    rows = grad_out.shape[0]
    moves = [
        pltpu.make_async_copy(sums.at[pl.ds(start, out.shape[0])], out, sems.at[i])
        for i, (start, out) in enumerate(
            ((rows, grad_in), (0, grad_out), (3 * rows, grad_trunk))
        )
    ]
    for move in moves:
        move.start()
    for move in moves:
        move.wait()


def fused_step(
    n,
    sensor_values,
    amplitude,
    field_modes,
    point_index,
    forcing,
    branch_in,
    branch_in_bias,
    branch_out,
    branch_out_bias,
    trunk_in,
    trunk_in_bias,
    trunk_out,
    trunk_out_bias,
):
    f32, bf16 = jnp.float32, jnp.bfloat16
    width = trunk_out.shape[1]
    own = point_index.shape[0]
    npts = own * n
    out_rows = width // n
    rows = PIECE
    pieces = 4 * out_rows // rows
    nz = n // 4
    row = lambda array: array.reshape(1, array.shape[0])
    operands = (
        sensor_values,
        row(amplitude),
        field_modes.T,
        point_index.T,
        row(forcing),
        branch_in,
        row(branch_in_bias),
        branch_out,
        row(branch_out_bias),
        trunk_in,
        row(trunk_in_bias),
        trunk_out,
        row(trunk_out_bias),
    )
    hbm = pl.BlockSpec(memory_space=pl.ANY)
    vmem = pl.BlockSpec(memory_space=pltpu.VMEM)
    sums = pl.pallas_call(
        functools.partial(step_kernel, n),
        out_shape=jax.ShapeDtypeStruct((4 * out_rows, width), f32),
        in_specs=[pl.BlockSpec(memory_space=pltpu.HBM)] * len(operands),
        out_specs=vmem,
        scratch_shapes=[pltpu.VMEM(array.shape, array.dtype) for array in operands]
        + [
            pltpu.VMEM((n, own, 128), f32),
            pltpu.VMEM((4 * npts, width), bf16),
            pltpu.VMEM((4 * npts, width), bf16),
            pltpu.VMEM((pieces, n, rows, width), bf16),
            pltpu.VMEM((pieces, n, rows, width), f32),
            pltpu.VMEM((pieces, nz, rows, width), bf16),
            pltpu.VMEM((pieces, nz, rows, width), f32),
            pltpu.VMEM((pieces, nz - 1, rows, width), bf16),
            pltpu.VMEM((pieces, n // 2, rows, width), bf16),
            pltpu.VMEM((pieces, nz, rows, width), bf16),
            pltpu.VMEM((pieces, nz - 1, rows, width), bf16),
            pltpu.VMEM((len(Z_FIRST), nz - 1, 2, rows, width), bf16),
            pltpu.VMEM((len(Z_FIRST), nz - 1, 2, rows, width), bf16),
            pltpu.VMEM((len(Z_FIRST), rows, width), bf16),
            pltpu.VMEM((len(Z_FIRST), rows, width), bf16),
            pltpu.SemaphoreType.DMA((len(operands),)),
            pltpu.SemaphoreType.DMA((n - 1,)),
            pltpu.SemaphoreType.DMA((n - 1,)),
            pltpu.SemaphoreType.DMA((pieces,)),
            pltpu.SemaphoreType.DMA((pieces,)),
            pltpu.SemaphoreType.DMA((pieces,)),
            pltpu.SemaphoreType.DMA((pieces,)),
            pltpu.SemaphoreType.DMA((pieces, nz - 1)),
            pltpu.SemaphoreType.DMA((pieces, nz - 1)),
        ],
        compiler_params=pltpu.CompilerParams(
            collective_id=0, has_side_effects=True, vmem_limit_bytes=60 * 2**20
        ),
    )(*operands)
    return pl.pallas_call(
        split_kernel,
        out_shape=(
            jax.ShapeDtypeStruct((2 * out_rows, width), f32),
            jax.ShapeDtypeStruct((out_rows, width), f32),
            jax.ShapeDtypeStruct((out_rows, width), f32),
        ),
        in_specs=[vmem],
        out_specs=(hbm, hbm, hbm),
        scratch_shapes=[pltpu.SemaphoreType.DMA((3,))],
    )(sums)


def device_step(n, *arrays):
    sensor_values, point_index, trunk_out = arrays[0], arrays[3], arrays[11]
    rows = trunk_out.shape[1] // n
    fits = (
        n % 4 == 0
        and n >= 8
        and rows % 16 == 0
        and point_index.shape[0] == 8
        and point_index.shape[0] * n == 128
        and sensor_values.shape[1] == 2 * rows * n
        and trunk_out.shape[0] == trunk_out.shape[1]
    )
    if fits:
        return fused_step(n, *arrays)
    return per_device(*arrays)


def solution(mesh):
    return jax.shard_map(
        functools.partial(device_step, mesh.shape["fn"]),
        mesh=mesh,
        in_specs=(
            P(("ens", "fn"), None),
            P(("ens", "fn")),
            P(("ens", "fn"), None),
            P(("ens", "fn"), None),
            P(("ens", "fn")),
            P(),
            P(),
            P(),
            P(),
            P(),
            P(),
            P(),
            P(),
        ),
        out_specs=(P(("ens", "fn"), None), P(("ens", "fn"), None), P(("ens", "fn"), None)),
        check_vma=False,
    )
```
